32 devices in a mesh: col: 4 (over y, x), row: 2 (over core), leaf: 4 (over z).
Axes of the slice: x: 2, y: 2, z: 4, core: 2. Of those that a mesh axis runs over, the one named last changes fastest.
Arguments:
- rhs_top: float32 [4, 4, 32, 1024], P(None, 'col', None, 'row'), may hold values from -6 to 6
- diag_inv: bfloat16 [4, 4, 1024, 1024], P(None, 'col', 'row'), may hold values from -1 to 1.25, as said below
- tile_vals: bfloat16 [4, 4, 2, 8, 4, 128, 128], P(None, 'col', None, 'row'), may hold values from -0.1875 to 0.1875
- tile_pattern: int32 [4, 4, 2, 8, 4], P(None, 'col', None, 'row'), may hold values from 0 to 7, as said below
- sub_vals: bfloat16 [4, 4, 2, 8, 4, 128, 128], P('col', 'leaf', None, 'row'), may hold values from -0.1875 to 0.1875
- sub_pattern: int32 [4, 4, 2, 8, 4], P('col', 'leaf', None, 'row'), may hold values from 0 to 7, as said below
- sub_solved: bfloat16 [4, 4, 32, 1024], P('col', 'leaf'), may hold values from -6 to 6
Outputs:
- solved: float32 [4, 4, 32, 1024], P(None, 'col', None, 'row')
- outgoing: float32 [4, 2, 32, 1024], P('col', None, None, 'row')
The draws below stay inside these ranges and needn't reach their ends.
Inputs may be any that keep to these rules, and one draw needn't show every extreme that they name: `tile_pattern`: in each row block of a panel tile the 4 column blocks are distinct. `sub_pattern`: in each row block of a subtree tile the 4 column blocks are distinct. `diag_inv`: lower triangular.
All inputs are finite; a program needn't handle non-finite values.
Results may differ from the reference program's by a relative error of at most 0.012.
Values may be sent and summed in bfloat16 or wider, within the bound.
A program may use at most 64 MiB of HBM per device.

```python
import math
import jax
import jax.numpy as jnp
from jax import lax

PW = 1024
SW = 1024
BLK = 128
NRHS = 32
STEPS = 4
KB = 8
NB = 4
KBS = 8
NBS = 4
N_COL = 4
N_LEAF = 4


def draw_diag_inv(key, part):
    key_diag, key_lower = jax.random.split(key)
    diagonal = jnp.exp(jax.random.uniform(key_diag, (STEPS, N_COL, PW), jnp.float32, math.log(0.8), math.log(1.25)))
    spread = 1.04 / math.sqrt(PW)
    lower = jax.random.uniform(key_lower, (STEPS, N_COL, PW, PW), jnp.float32, -spread, spread)
    rows = lax.broadcasted_iota(jnp.int32, (PW, PW), 0)
    columns = lax.broadcasted_iota(jnp.int32, (PW, PW), 1)
    matrix = jnp.where(rows > columns, lower, 0.0) + jnp.where(rows == columns, 1.0, 0.0) * diagonal[..., None]
    return matrix.astype(jnp.bfloat16)


def distinct_blocks(key, lead, total, keep):
    scores = jax.random.randint(key, lead + (total,), 0, 1 << 20) * total
    scores = scores + lax.broadcasted_iota(jnp.int32, lead + (total,), len(lead))
    order = jnp.argsort(scores, axis=-1)
    return order[..., :keep].astype(jnp.int32)


def draw_tile_pattern(key, part):
    return distinct_blocks(jax.random.fold_in(key, 11), (STEPS, N_COL, 2, KB), KB, NB)


def draw_sub_pattern(key, part):
    return distinct_blocks(jax.random.fold_in(key, 23), (N_COL, N_LEAF, 2, KB), KBS, NBS)


def levels(own_key, dims, shards, low, largest):
    loudness = 1.0
    for dim, parts in shards:
        steps = jax.random.uniform(jax.random.fold_in(jax.random.fold_in(own_key, 6), dim), (parts,), jnp.float32, low / len(shards), largest / len(shards))
        loudness = loudness * jnp.repeat(jnp.exp(steps), dims[dim] // parts).reshape((-1,) + (1,) * (len(dims) - 1 - dim))
    return loudness


def scatter_about(rng, dims, scale, limit, shards=(), dtype=jnp.bfloat16):
    drawn = jax.random.normal(rng, dims, jnp.float32) * scale
    if len(shards) > 0:
        drawn = levels(rng, dims, shards, -0.22, 0.18) * drawn
    return jnp.clip(drawn, min=-limit, max=limit).astype(dtype)


def setup_inputs(seed: int = 0) -> dict:
    seeds = jax.random.split(jax.random.key(seed), 8)
    return {
        "rhs_top": scatter_about(seeds[0], (STEPS, N_COL, NRHS, PW), 1.0, 6.0, ((1, 4), (3, 2)), jnp.float32),
        "diag_inv": draw_diag_inv(jax.random.fold_in(seeds[7], 71), 0),
        "tile_vals": scatter_about(seeds[2], (STEPS, N_COL, 2, KB, NB, BLK, BLK), PW ** -0.5, 0.1875, ((1, 4), (3, 2))),
        "tile_pattern": draw_tile_pattern(jax.random.fold_in(seeds[7], 71), 0),
        "sub_vals": scatter_about(seeds[4], (N_COL, N_LEAF, 2, KB, NBS, BLK, BLK), SW ** -0.5, 0.1875, ((0, 4), (1, 4), (3, 2))),
        "sub_pattern": draw_sub_pattern(jax.random.fold_in(seeds[7], 71), 0),
        "sub_solved": scatter_about(seeds[6], (N_COL, N_LEAF, NRHS, SW), 1.0, 6.0, ((0, 4), (1, 4))),
    }


def blocked_product(vectors, values, pattern):
    count, nrows, width = vectors.shape
    blocks = vectors.reshape(count, nrows, width // BLK, BLK).transpose(0, 2, 1, 3)
    chosen = jax.vmap(lambda blk_rows, pat: blk_rows[pat])(blocks, pattern)
    result = jnp.einsum("nhbkri,nhbkij->nhrbj", chosen.astype(jnp.float32), values.astype(jnp.float32))
    return result.reshape(count, 2, nrows, PW)


def reference(rhs_top, diag_inv, tile_vals, tile_pattern, sub_vals, sub_pattern, sub_solved):
    flat_vals = sub_vals.reshape((N_COL * N_LEAF,) + sub_vals.shape[2:])
    flat_pattern = sub_pattern.reshape((N_COL * N_LEAF,) + sub_pattern.shape[2:])
    flat_solved = sub_solved.reshape((N_COL * N_LEAF,) + sub_solved.shape[2:])
    partial_value = blocked_product(flat_solved, flat_vals, flat_pattern)
    carry = jnp.sum(partial_value.reshape(N_COL, N_LEAF, 2, NRHS, PW), axis=1)
    outputs = []
    for level in range(STEPS):
        rhs = rhs_top[level] - carry[:, 0]
        rhs_b = rhs.astype(jnp.bfloat16)
        solved = jnp.einsum("cri,cji->crj", rhs_b.astype(jnp.float32), diag_inv[level].astype(jnp.float32))
        outputs.append(solved)
        solved_b = solved.astype(jnp.bfloat16)
        update = blocked_product(solved_b, tile_vals[level], tile_pattern[level])
        sent = jnp.stack([update[:, 0] + carry[:, 1], update[:, 1]], axis=1)
        carry = jnp.roll(sent, 1, axis=0)
    return jnp.stack(outputs, axis=0), carry
```

```python
import functools

import jax
import jax.numpy as jnp
from jax import lax
from jax.experimental import pallas as pl
from jax.experimental.pallas import tpu as pltpu
from jax.sharding import PartitionSpec as P

MESH = pl.DeviceIdType.MESH
F32 = jnp.float32
BF16 = jnp.bfloat16


def pack(x):
    half = x.shape[1] // 2
    return jnp.concatenate([x[:, :half], x[:, half:]], axis=0)


def kernel(
    sizes,
    rhs_hbm,
    diag_hbm,
    tile_hbm,
    tile_pat,
    sub_hbm,
    sub_pat,
    subx_hbm,
    solved_out,
    outgoing,
    subv,
    subx,
    subx3,
    tiles,
    diag,
    rhs0,
    rhsn,
    part_send,
    part0,
    part1,
    xmsg,
    xsend,
    cmsg,
    csend,
    sx3,
    sol,
    fin,
    load_sem,
    send_sem,
    part0_sem,
    part1_sem,
    diag_sem,
    rhs_sem,
    x_sem,
    c_sem,
    sol_sem,
    fin_sem,
):
    C, R, L, G, S, NRHS, W, BLK, NBR, NB = sizes
    m = NRHS // G
    c, r, l = lax.axis_index("col"), lax.axis_index("row"), lax.axis_index("leaf")
    g = lax.rem(l, G)
    base = l - g
    nxt, prv = lax.rem(c + 1, C), lax.rem(c + C - 1, C)
    rows = pl.ds(pl.multiple_of(g * m, m), m)
    started = []

    def leaf_at(d):
        return lax.rem(l + d, L)

    def row_at(d):
        return lax.rem(r + d, R)

    def mate(d):
        return base + lax.rem(g + d, G)

    loads = []

    def load(src, dst):
        copy = pltpu.make_async_copy(src, dst, load_sem.at[len(loads)])
        copy.start()
        loads.append(copy)
        return copy

    def send(src, dst, sem, target):
        copy = pltpu.make_async_remote_copy(
            src_ref=src,
            dst_ref=dst,
            send_sem=send_sem.at[len(started)],
            recv_sem=sem,
            device_id=target,
            device_id_type=MESH,
        )
        copy.start()
        started.append(copy)

    def arrived(dst, sem):
        pltpu.make_async_remote_copy(
            src_ref=dst,
            dst_ref=dst,
            send_sem=send_sem.at[0],
            recv_sem=sem,
            device_id=(c, r, l),
            device_id_type=MESH,
        ).wait_recv()

    barrier = pltpu.get_barrier_semaphore()
    peers = []
    for dl in range(L):
        for dr in range(R):
            if dl or dr:
                peers.append((c, row_at(dr), leaf_at(dl)))
    for other in (nxt, prv):
        for dr in range(R):
            peers.append((other, row_at(dr), l))
        for d in range(1, G):
            peers.append((other, r, mate(d)))
    for peer in peers:
        pl.semaphore_signal(barrier, inc=1, device_id=peer, device_id_type=MESH)

    load_x = load(subx_hbm.at[0, 0], subx)
    load_v = load(sub_hbm.at[0, 0], subv)
    load_r = load(rhs_hbm.at[0, 0, rows], rhs0.at[r])
    load_d, load_t = [], []
    for s in range(S):
        load_d.append(load(diag_hbm.at[s, 0], diag.at[s, r]))
        load_t.append(load(tile_hbm.at[s, 0], tiles.at[s]))

    pl.semaphore_wait(barrier, len(peers))

    for dr in range(1, R):
        send(rhs_hbm.at[0, 0, rows], rhs0.at[r], rhs_sem.at[r], (c, row_at(dr), l))
        send(diag_hbm.at[0, 0], diag.at[0, r], diag_sem.at[0, r], (c, row_at(dr), l))
    send(rhs_hbm.at[pl.ds(1, S - 1), 0, rows], rhsn, rhs_sem.at[R], (prv, r, l))

    def product(lookup, pat, vals):
        lhs = jnp.concatenate([lookup(pat(k)) for k in range(NB)], axis=1)
        return jnp.dot(lhs.astype(BF16), vals[...].reshape(NB * BLK, BLK), preferred_element_type=F32)

    load_x.wait()
    for k in range(subx3.shape[0]):
        subx3[k] = subx[:, k * BLK : (k + 1) * BLK]
    load_v.wait()
    for h in range(2):
        part = jnp.concatenate(
            [
                product(lambda i: subx3[i], lambda k: sub_pat[0, 0, h, b, k], subv.at[h, b])
                for b in range(NBR)
            ],
            axis=1,
        )
        for j in range(G):
            part_send[h, j] = pack(part[j * m : (j + 1) * m]).astype(BF16)
        if h == 0:
            part0[l, r] = part_send[0, g]
            for dl in range(L):
                for dr in range(R):
                    if dl or dr:
                        there = leaf_at(dl)
                        send(
                            part_send.at[0, lax.rem(there, G)],
                            part0.at[l, r],
                            part0_sem.at[l, r],
                            (c, row_at(dr), there),
                        )
        else:
            part1[l] = part_send[1, g]
            for dl in range(1, L):
                there = leaf_at(dl)
                send(part_send.at[1, lax.rem(there, G)], part1.at[l], part1_sem.at[l], (c, r, there))
    for s in range(1, S):
        for dr in range(1, R):
            send(diag_hbm.at[s, 0], diag.at[s, r], diag_sem.at[s, r], (c, row_at(dr), l))

    load_r.wait()
    for dr in range(1, R):
        there = row_at(dr)
        arrived(rhs0.at[there], rhs_sem.at[there])
    for dl in range(L):
        for dr in range(R):
            if dl or dr:
                i, j = leaf_at(dl), row_at(dr)
                arrived(part0.at[i, j], part0_sem.at[i, j])
    pieces = []
    for j in range(R):
        total = part0[0, j].astype(F32)
        for i in range(1, L):
            total = total + part0[i, j].astype(F32)
        value = pack(rhs0[j]) - total
        pieces += [value[:m], value[m:]]

    for s in range(S):
        if s > 0:
            pieces = []
            for j in range(R):
                arrived(xmsg.at[s - 1, j], x_sem.at[s - 1, j])
                value = xmsg[s - 1, j].astype(F32)
                pieces += [value[:m], value[m:]]
        x = jnp.concatenate(pieces, axis=1).astype(BF16)
        load_d[s].wait()
        for dr in range(1, R):
            there = row_at(dr)
            arrived(diag.at[s, there], diag_sem.at[s, there])
        step = W // 2
        for i in range(2 * R):
            reach = (i + 1) * step
            block = lax.dot_general(
                x[:, :reach],
                diag[s, i // 2, (i % 2) * step : (i % 2 + 1) * step, :reach],
                (((1,), (1,)), ((), ())),
                preferred_element_type=F32,
            )
            sol[s, i // 2, :, (i % 2) * step : (i % 2 + 1) * step] = block
            for k in range(step // BLK):
                sx3[s, i * (step // BLK) + k] = block[:, k * BLK : (k + 1) * BLK]

        load_t[s].wait()

        def update(h):
            return jnp.concatenate(
                [
                    product(lambda i: sx3[s, i], lambda k: tile_pat[s, 0, h, b, k], tiles.at[s, h, b])
                    for b in range(NBR)
                ],
                axis=1,
            )

        def carried():
            if s > 0:
                arrived(cmsg.at[s - 1], c_sem.at[s - 1])
                return cmsg[s - 1]
            for dl in range(1, L):
                i = leaf_at(dl)
                arrived(part1.at[i], part1_sem.at[i])
            total = part1[0].astype(F32)
            for i in range(1, L):
                total = total + part1[i].astype(F32)
            return jnp.concatenate([total[:m], total[m:]], axis=1)

        if s < S - 1:
            if s == 0:
                arrived(rhsn, rhs_sem.at[R])
            first = rhsn[s] - (update(0) + carried())
            xsend[s] = pack(first).astype(BF16)
            for dr in range(R):
                send(xsend.at[s], xmsg.at[s, r], x_sem.at[s, r], (nxt, row_at(dr), l))
            csend[s] = update(1)
            send(csend.at[s], cmsg.at[s], c_sem.at[s], (nxt, r, l))
        load(sol.at[s, r], solved_out.at[s, 0, rows])
        for d in range(1, G):
            send(sol.at[s, r], solved_out.at[s, 0, rows], sol_sem.at[s, g], (c, r, mate(d)))
        if s == S - 1:
            for h in range(2):
                fin[h] = update(h) + carried() if h == 0 else update(h)
                for d in range(G):
                    send(fin.at[h], outgoing.at[0, h, rows], fin_sem.at[h, g], (nxt, r, mate(d)))

    for s in range(S):
        for d in range(1, G):
            j = lax.rem(g + d, G)
            there = pl.ds(pl.multiple_of(j * m, m), m)
            arrived(solved_out.at[s, 0, there], sol_sem.at[s, j])
    for h in range(2):
        for j in range(G):
            arrived(outgoing.at[0, h, pl.ds(j * m, m)], fin_sem.at[h, j])
    for copy in loads[-S:]:
        copy.wait()
    for copy in started:
        copy.wait_send()


def per_device(axes, rhs_top, diag_inv, tile_vals, tile_pattern, sub_vals, sub_pattern, sub_solved):
    C, R, L = axes
    S, _, NRHS, W = rhs_top.shape
    NBR, NB, BLK = tile_vals.shape[3:6]
    PW = diag_inv.shape[3]
    SW = sub_solved.shape[3]
    G = max(1, min(L, NRHS // 8))
    m = NRHS // G
    sizes = (C, R, L, G, S, NRHS, W, BLK, NBR, NB)
    hbm = pl.BlockSpec(memory_space=pltpu.HBM)
    out = pl.BlockSpec(memory_space=pl.ANY)
    smem = pl.BlockSpec(memory_space=pltpu.SMEM)
    dma = pltpu.SemaphoreType.DMA
    n_sends = (
        2 * (R - 1) + 1 + (L * R - 1) + (L - 1) + (S - 1) * (R - 1) + (S - 1) * (R + 1) + S * (G - 1) + 2 * G
    )
    return pl.pallas_call(
        functools.partial(kernel, sizes),
        out_shape=(
            jax.ShapeDtypeStruct((S, 1, NRHS, W), F32),
            jax.ShapeDtypeStruct((1, 2, NRHS, W), F32),
        ),
        in_specs=[hbm, hbm, hbm, smem, hbm, smem, hbm],
        out_specs=(out, out),
        scratch_shapes=[
            pltpu.VMEM(sub_vals.shape[2:], BF16),
            pltpu.VMEM((NRHS, SW), BF16),
            pltpu.VMEM((SW // BLK, NRHS, BLK), BF16),
            pltpu.VMEM((S,) + tile_vals.shape[2:], BF16),
            pltpu.VMEM((S, R, W, PW), BF16),
            pltpu.VMEM((R, m, W), F32),
            pltpu.VMEM((S - 1, m, W), F32),
            pltpu.VMEM((2, G, 2 * m, W // 2), BF16),
            pltpu.VMEM((L, R, 2 * m, W // 2), BF16),
            pltpu.VMEM((L, 2 * m, W // 2), BF16),
            pltpu.VMEM((S - 1, R, 2 * m, W // 2), BF16),
            pltpu.VMEM((S - 1, 2 * m, W // 2), BF16),
            pltpu.VMEM((S - 1, m, W), F32),
            pltpu.VMEM((S - 1, m, W), F32),
            pltpu.VMEM((S, PW // BLK, m, BLK), F32),
            pltpu.VMEM((S, R, m, W), F32),
            pltpu.VMEM((2, m, W), F32),
            dma((3 + 3 * S,)),
            dma((n_sends,)),
            dma((L, R)),
            dma((L,)),
            dma((S, R)),
            dma((R + 1,)),
            dma((S - 1, R)),
            dma((S - 1,)),
            dma((S, G)),
            dma((2, G)),
        ],
        compiler_params=pltpu.CompilerParams(
            collective_id=0, has_side_effects=True, vmem_limit_bytes=48 * 1024 * 1024
        ),
    )(rhs_top, diag_inv, tile_vals, tile_pattern, sub_vals, sub_pattern, sub_solved)


def solution(mesh):
    placed = (
        P(None, "col", None, "row"),
        P(None, "col", "row", None),
        P(None, "col", None, "row", None, None, None),
        P(None, "col", None, "row", None),
        P("col", "leaf", None, "row", None, None, None),
        P("col", "leaf", None, "row", None),
        P("col", "leaf", None, None),
    )
    axes = tuple(mesh.shape[name] for name in ("col", "row", "leaf"))
    return jax.shard_map(
        functools.partial(per_device, axes),
        mesh=mesh,
        in_specs=placed,
        out_specs=(P(None, "col", None, "row"), P("col", None, None, "row")),
        check_vma=False,
    )
```

```python
import functools

import jax
import jax.numpy as jnp
from jax import lax
from jax.experimental import pallas as pl
from jax.experimental.pallas import tpu as pltpu
from jax.sharding import PartitionSpec as P

MESH = pl.DeviceIdType.MESH
F32 = jnp.float32
BF16 = jnp.bfloat16


def pack(x):
    half = x.shape[1] // 2
    return jnp.concatenate([x[:, :half], x[:, half:]], axis=0)


def kernel(
    sizes,
    rhs_hbm,
    diag_hbm,
    tile_hbm,
    tile_pat,
    sub_hbm,
    sub_pat,
    subx_hbm,
    solved_all,
    fin_all,
    subv,
    subx,
    subx3,
    tiles,
    diag,
    rhs0,
    rhsn,
    part_send,
    part0,
    part1,
    xmsg,
    xsend,
    cmsg,
    csend,
    sx3,
    sol,
    fin,
    load_sem,
    send_sem,
    part0_sem,
    part1_sem,
    diag_sem,
    rhs_sem,
    x_sem,
    c_sem,
    sol_sem,
    fin_sem,
):
    C, R, L, G, S, NRHS, W, BLK, NBR, NB = sizes
    m = NRHS // G
    c, r, l = lax.axis_index("col"), lax.axis_index("row"), lax.axis_index("leaf")
    g = lax.rem(l, G)
    base = l - g
    nxt, prv = lax.rem(c + 1, C), lax.rem(c + C - 1, C)
    rows = pl.ds(pl.multiple_of(g * m, m), m)
    started = []

    def leaf_at(d):
        return lax.rem(l + d, L)

    def row_at(d):
        return lax.rem(r + d, R)

    def mate(d):
        return base + lax.rem(g + d, G)

    loads = []

    def load(src, dst):
        copy = pltpu.make_async_copy(src, dst, load_sem.at[len(loads)])
        copy.start()
        loads.append(copy)
        return copy

    def send(src, dst, sem, target):
        copy = pltpu.make_async_remote_copy(
            src_ref=src,
            dst_ref=dst,
            send_sem=send_sem.at[len(started)],
            recv_sem=sem,
            device_id=target,
            device_id_type=MESH,
        )
        copy.start()
        started.append(copy)

    def arrived(dst, sem):
        pltpu.make_async_remote_copy(
            src_ref=dst,
            dst_ref=dst,
            send_sem=send_sem.at[0],
            recv_sem=sem,
            device_id=(c, r, l),
            device_id_type=MESH,
        ).wait_recv()

    barrier = pltpu.get_barrier_semaphore()
    peers = []
    for dl in range(L):
        for dr in range(R):
            if dl or dr:
                peers.append((c, row_at(dr), leaf_at(dl)))
    for other in (nxt, prv):
        for dr in range(R):
            peers.append((other, row_at(dr), l))
    for peer in peers:
        pl.semaphore_signal(barrier, inc=1, device_id=peer, device_id_type=MESH)

    load_x = load(subx_hbm.at[0, 0], subx)
    load_v = load(sub_hbm.at[0, 0], subv)
    load_r = load(rhs_hbm.at[0, 0, rows], rhs0.at[r])
    load_d, load_t = [], []
    for s in range(S):
        load_d.append(load(diag_hbm.at[s, 0], diag.at[s, r]))
        load_t.append(load(tile_hbm.at[s, 0], tiles.at[s]))

    def product(lookup, pat, vals):
        lhs = jnp.concatenate([lookup(pat(k)) for k in range(NB)], axis=1)
        return jnp.dot(lhs.astype(BF16), vals[...].reshape(NB * BLK, BLK), preferred_element_type=F32)

    load_x.wait()
    for k in range(subx3.shape[0]):
        subx3[k] = subx[:, k * BLK : (k + 1) * BLK]
    load_v.wait()
    for h in range(2):
        part = jnp.concatenate(
            [
                product(lambda i: subx3[i], lambda k: sub_pat[0, 0, h, b, k], subv.at[h, b])
                for b in range(NBR)
            ],
            axis=1,
        )
        for j in range(G):
            part_send[h, j] = pack(part[j * m : (j + 1) * m]).astype(BF16)
    part0[l, r] = part_send[0, g]
    part1[l] = part_send[1, g]

    pl.semaphore_wait(barrier, len(peers))

    for dr in range(1, R):
        send(rhs_hbm.at[0, 0, rows], rhs0.at[r], rhs_sem.at[r], (c, row_at(dr), l))
    for dl in range(L):
        for dr in range(R):
            if dl or dr:
                there = leaf_at(dl)
                send(
                    part_send.at[0, lax.rem(there, G)],
                    part0.at[l, r],
                    part0_sem.at[l, r],
                    (c, row_at(dr), there),
                )
    for dr in range(1, R):
        send(diag_hbm.at[0, 0], diag.at[0, r], diag_sem.at[0, r], (c, row_at(dr), l))
    for dl in range(1, L):
        there = leaf_at(dl)
        send(part_send.at[1, lax.rem(there, G)], part1.at[l], part1_sem.at[l], (c, r, there))
    send(rhs_hbm.at[pl.ds(1, S - 1), 0, rows], rhsn, rhs_sem.at[R], (prv, r, l))
    for s in range(1, S):
        for dr in range(1, R):
            send(diag_hbm.at[s, 0], diag.at[s, r], diag_sem.at[s, r], (c, row_at(dr), l))

    load_r.wait()
    for dr in range(1, R):
        there = row_at(dr)
        arrived(rhs0.at[there], rhs_sem.at[there])
    for dl in range(L):
        for dr in range(R):
            if dl or dr:
                i, j = leaf_at(dl), row_at(dr)
                arrived(part0.at[i, j], part0_sem.at[i, j])
    pieces = []
    for j in range(R):
        total = part0[0, j].astype(F32)
        for i in range(1, L):
            total = total + part0[i, j].astype(F32)
        value = pack(rhs0[j]) - total
        pieces += [value[:m], value[m:]]

    for s in range(S):
        if s > 0:
            pieces = []
            for j in range(R):
                arrived(xmsg.at[s - 1, j], x_sem.at[s - 1, j])
                value = xmsg[s - 1, j].astype(F32)
                pieces += [value[:m], value[m:]]
        x = jnp.concatenate(pieces, axis=1).astype(BF16)
        load_d[s].wait()
        for dr in range(1, R):
            there = row_at(dr)
            arrived(diag.at[s, there], diag_sem.at[s, there])
        step = W // 2
        for i in range(2 * R):
            reach = (i + 1) * step
            block = lax.dot_general(
                x[:, :reach],
                diag[s, i // 2, (i % 2) * step : (i % 2 + 1) * step, :reach],
                (((1,), (1,)), ((), ())),
                preferred_element_type=F32,
            )
            sol[s, i // 2, :, (i % 2) * step : (i % 2 + 1) * step] = block
            for k in range(step // BLK):
                sx3[s, i * (step // BLK) + k] = block[:, k * BLK : (k + 1) * BLK]

        load_t[s].wait()

        def update(h):
            return jnp.concatenate(
                [
                    product(lambda i: sx3[s, i], lambda k: tile_pat[s, 0, h, b, k], tiles.at[s, h, b])
                    for b in range(NBR)
                ],
                axis=1,
            )

        def carried():
            if s > 0:
                arrived(cmsg.at[s - 1], c_sem.at[s - 1])
                return cmsg[s - 1]
            for dl in range(1, L):
                i = leaf_at(dl)
                arrived(part1.at[i], part1_sem.at[i])
            total = part1[0].astype(F32)
            for i in range(1, L):
                total = total + part1[i].astype(F32)
            return jnp.concatenate([total[:m], total[m:]], axis=1)

        if s < S - 1:
            if s == 0:
                arrived(rhsn, rhs_sem.at[R])
            first = rhsn[s] - (update(0) + carried())
            xsend[s] = pack(first).astype(BF16)
            for dr in range(R):
                send(xsend.at[s], xmsg.at[s, r], x_sem.at[s, r], (nxt, row_at(dr), l))
            csend[s] = update(1)
            send(csend.at[s], cmsg.at[s], c_sem.at[s], (nxt, r, l))
        solved_all[s, g] = pack(sol[s, r]).astype(BF16)
        for d in range(1, G):
            send(solved_all.at[s, g], solved_all.at[s, g], sol_sem.at[s, g], (c, r, mate(d)))
        if s == S - 1:
            for h in range(2):
                fin[h] = pack(update(h) + carried() if h == 0 else update(h)).astype(BF16)
                for d in range(G):
                    send(fin.at[h], fin_all.at[h, g], fin_sem.at[h, g], (nxt, r, mate(d)))

    for s in range(S):
        for d in range(1, G):
            j = lax.rem(g + d, G)
            arrived(solved_all.at[s, j], sol_sem.at[s, j])
    for h in range(2):
        for j in range(G):
            arrived(fin_all.at[h, j], fin_sem.at[h, j])
    for copy in started:
        copy.wait_send()


def unpack_kernel(m, solved_all, fin_all, solved_out, outgoing):
    half = solved_all.shape[3]
    for i in range(solved_all.shape[0]):
        for j in range(solved_all.shape[1]):
            value = solved_all[i, j].astype(F32)
            solved_out[i, 0, j * m : (j + 1) * m, :half] = value[:m]
            solved_out[i, 0, j * m : (j + 1) * m, half:] = value[m:]
    for i in range(fin_all.shape[0]):
        for j in range(fin_all.shape[1]):
            value = fin_all[i, j].astype(F32)
            outgoing[0, i, j * m : (j + 1) * m, :half] = value[:m]
            outgoing[0, i, j * m : (j + 1) * m, half:] = value[m:]


def per_device(axes, rhs_top, diag_inv, tile_vals, tile_pattern, sub_vals, sub_pattern, sub_solved):
    C, R, L = axes
    S, _, NRHS, W = rhs_top.shape
    NBR, NB, BLK = tile_vals.shape[3:6]
    PW = diag_inv.shape[3]
    SW = sub_solved.shape[3]
    G = max(1, min(L, NRHS // 8))
    m = NRHS // G
    sizes = (C, R, L, G, S, NRHS, W, BLK, NBR, NB)
    hbm = pl.BlockSpec(memory_space=pltpu.HBM)
    out = pl.BlockSpec(memory_space=pltpu.VMEM)
    smem = pl.BlockSpec(memory_space=pltpu.SMEM)
    dma = pltpu.SemaphoreType.DMA
    n_sends = (
        2 * (R - 1) + 1 + (L * R - 1) + (L - 1) + (S - 1) * (R - 1) + (S - 1) * (R + 1) + S * (G - 1) + 2 * G
    )
    solved_all, fin_all = pl.pallas_call(
        functools.partial(kernel, sizes),
        out_shape=(
            jax.ShapeDtypeStruct((S, G, 2 * m, W // 2), BF16),
            jax.ShapeDtypeStruct((2, G, 2 * m, W // 2), BF16),
        ),
        in_specs=[hbm, hbm, hbm, smem, hbm, smem, hbm],
        out_specs=(out, out),
        scratch_shapes=[
            pltpu.VMEM(sub_vals.shape[2:], BF16),
            pltpu.VMEM((NRHS, SW), BF16),
            pltpu.VMEM((SW // BLK, NRHS, BLK), BF16),
            pltpu.VMEM((S,) + tile_vals.shape[2:], BF16),
            pltpu.VMEM((S, R, W, PW), BF16),
            pltpu.VMEM((R, m, W), F32),
            pltpu.VMEM((S - 1, m, W), F32),
            pltpu.VMEM((2, G, 2 * m, W // 2), BF16),
            pltpu.VMEM((L, R, 2 * m, W // 2), BF16),
            pltpu.VMEM((L, 2 * m, W // 2), BF16),
            pltpu.VMEM((S - 1, R, 2 * m, W // 2), BF16),
            pltpu.VMEM((S - 1, 2 * m, W // 2), BF16),
            pltpu.VMEM((S - 1, m, W), F32),
            pltpu.VMEM((S - 1, m, W), F32),
            pltpu.VMEM((S, PW // BLK, m, BLK), F32),
            pltpu.VMEM((S, R, m, W), F32),
            pltpu.VMEM((2, 2 * m, W // 2), BF16),
            dma((3 + 2 * S,)),
            dma((n_sends,)),
            dma((L, R)),
            dma((L,)),
            dma((S, R)),
            dma((R + 1,)),
            dma((S - 1, R)),
            dma((S - 1,)),
            dma((S, G)),
            dma((2, G)),
        ],
        compiler_params=pltpu.CompilerParams(
            collective_id=0, has_side_effects=True, vmem_limit_bytes=56 * 1024 * 1024
        ),
    )(rhs_top, diag_inv, tile_vals, tile_pattern, sub_vals, sub_pattern, sub_solved)
    return pl.pallas_call(
        functools.partial(unpack_kernel, m),
        out_shape=(
            jax.ShapeDtypeStruct((S, 1, NRHS, W), F32),
            jax.ShapeDtypeStruct((1, 2, NRHS, W), F32),
        ),
        in_specs=[pl.BlockSpec(memory_space=pltpu.VMEM)] * 2,
        out_specs=(pl.BlockSpec(memory_space=pltpu.VMEM),) * 2,
    )(solved_all, fin_all)


def solution(mesh):
    placed = (
        P(None, "col", None, "row"),
        P(None, "col", "row", None),
        P(None, "col", None, "row", None, None, None),
        P(None, "col", None, "row", None),
        P("col", "leaf", None, "row", None, None, None),
        P("col", "leaf", None, "row", None),
        P("col", "leaf", None, None),
    )
    axes = tuple(mesh.shape[name] for name in ("col", "row", "leaf"))
    return jax.shard_map(
        functools.partial(per_device, axes),
        mesh=mesh,
        in_specs=placed,
        out_specs=(P(None, "col", None, "row"), P("col", None, None, "row")),
        check_vma=False,
    )
```

```python
import functools

import jax
import jax.numpy as jnp
from jax import lax
from jax.experimental import pallas as pl
from jax.experimental.pallas import tpu as pltpu
from jax.sharding import PartitionSpec as P

MESH = pl.DeviceIdType.MESH
F32 = jnp.float32
BF16 = jnp.bfloat16


def pack(x):
    half = x.shape[1] // 2
    return jnp.concatenate([x[:, :half], x[:, half:]], axis=0)


def kernel(
    sizes,
    rhs_hbm,
    diag_hbm,
    tile_hbm,
    tile_pat,
    sub_hbm,
    sub_pat,
    subx_hbm,
    solved_all,
    fin_all,
    subv,
    subx,
    subx3,
    tiles,
    diag,
    rhs0,
    rhsn,
    part_send,
    part0,
    part1,
    xmsg,
    xsend,
    cmsg,
    csend,
    sx3,
    sol,
    fin,
    mine,
    load_sem,
    send_sem,
    part0_sem,
    part1_sem,
    diag_sem,
    rhs_sem,
    x_sem,
    c_sem,
    sol_sem,
    fin_sem,
):
    C, R, L, G, S, NRHS, W, BLK, NBR, NB = sizes
    m = NRHS // G
    c, r, l = lax.axis_index("col"), lax.axis_index("row"), lax.axis_index("leaf")
    g = lax.rem(l, G)
    base = l - g
    nxt, prv = lax.rem(c + 1, C), lax.rem(c + C - 1, C)
    rows = pl.ds(pl.multiple_of(g * m, m), m)
    started = []

    def leaf_at(d):
        return lax.rem(l + d, L)

    def row_at(d):
        return lax.rem(r + d, R)

    def mate(d):
        return base + lax.rem(g + d, G)

    loads = []

    def load(src, dst):
        copy = pltpu.make_async_copy(src, dst, load_sem.at[len(loads)])
        copy.start()
        loads.append(copy)
        return copy

    def send(src, dst, sem, target):
        copy = pltpu.make_async_remote_copy(
            src_ref=src,
            dst_ref=dst,
            send_sem=send_sem.at[len(started)],
            recv_sem=sem,
            device_id=target,
            device_id_type=MESH,
        )
        copy.start()
        started.append(copy)

    def arrived(dst, sem):
        pltpu.make_async_remote_copy(
            src_ref=dst,
            dst_ref=dst,
            send_sem=send_sem.at[0],
            recv_sem=sem,
            device_id=(c, r, l),
            device_id_type=MESH,
        ).wait_recv()

    barrier = pltpu.get_barrier_semaphore()
    peers = []
    for dl in range(L):
        for dr in range(R):
            if dl or dr:
                peers.append((c, row_at(dr), leaf_at(dl)))
    for other in (nxt, prv):
        for dr in range(R):
            peers.append((other, row_at(dr), l))
    for peer in peers:
        pl.semaphore_signal(barrier, inc=1, device_id=peer, device_id_type=MESH)

    load_x = load(subx_hbm.at[0, 0], subx)
    load_v = load(sub_hbm.at[0, 0], subv)
    load_r = load(rhs_hbm.at[0, 0, rows], rhs0.at[r])
    load_d, load_t = [], []
    for s in range(S):
        load_d.append(load(diag_hbm.at[s, 0], diag.at[s, r]))
        load_t.append(load(tile_hbm.at[s, 0], tiles.at[s]))

    def product(lookup, pat, vals):
        lhs = jnp.concatenate([lookup(pat(k)) for k in range(NB)], axis=1)
        return jnp.dot(lhs.astype(BF16), vals[...].reshape(NB * BLK, BLK), preferred_element_type=F32)

    load_x.wait()
    for k in range(subx3.shape[0]):
        subx3[k] = subx[:, k * BLK : (k + 1) * BLK]
    load_v.wait()
    for h in range(2):
        part = jnp.concatenate(
            [
                product(lambda i: subx3[i], lambda k: sub_pat[0, 0, h, b, k], subv.at[h, b])
                for b in range(NBR)
            ],
            axis=1,
        )
        for j in range(G):
            part_send[h, j] = pack(part[j * m : (j + 1) * m]).astype(BF16)
    part0[l, r] = part_send[0, g]
    part1[l] = part_send[1, g]

    pl.semaphore_wait(barrier, len(peers))

    for dr in range(1, R):
        send(rhs_hbm.at[0, 0, rows], rhs0.at[r], rhs_sem.at[r], (c, row_at(dr), l))
    for dl in range(L):
        for dr in range(R):
            if dl or dr:
                there = leaf_at(dl)
                send(
                    part_send.at[0, lax.rem(there, G)],
                    part0.at[l, r],
                    part0_sem.at[l, r],
                    (c, row_at(dr), there),
                )
    for dr in range(1, R):
        send(diag_hbm.at[0, 0], diag.at[0, r], diag_sem.at[0, r], (c, row_at(dr), l))
    for dl in range(1, L):
        there = leaf_at(dl)
        send(part_send.at[1, lax.rem(there, G)], part1.at[l], part1_sem.at[l], (c, r, there))
    send(rhs_hbm.at[pl.ds(1, S - 1), 0, rows], rhsn, rhs_sem.at[R], (prv, r, l))
    for s in range(1, S):
        for dr in range(1, R):
            send(diag_hbm.at[s, 0], diag.at[s, r], diag_sem.at[s, r], (c, row_at(dr), l))

    load_r.wait()
    for dr in range(1, R):
        there = row_at(dr)
        arrived(rhs0.at[there], rhs_sem.at[there])
    for dl in range(L):
        for dr in range(R):
            if dl or dr:
                i, j = leaf_at(dl), row_at(dr)
                arrived(part0.at[i, j], part0_sem.at[i, j])
    pieces = []
    for j in range(R):
        total = part0[0, j].astype(F32)
        for i in range(1, L):
            total = total + part0[i, j].astype(F32)
        value = pack(rhs0[j]) - total
        pieces += [value[:m], value[m:]]

    for s in range(S):
        if s > 0:
            pieces = []
            for j in range(R):
                arrived(xmsg.at[s - 1, j], x_sem.at[s - 1, j])
                value = xmsg[s - 1, j].astype(F32)
                pieces += [value[:m], value[m:]]
        x = jnp.concatenate(pieces, axis=1).astype(BF16)
        load_d[s].wait()
        for dr in range(1, R):
            there = row_at(dr)
            arrived(diag.at[s, there], diag_sem.at[s, there])
        step = W // 2
        for i in range(2 * R):
            reach = (i + 1) * step
            block = lax.dot_general(
                x[:, :reach],
                diag[s, i // 2, (i % 2) * step : (i % 2 + 1) * step, :reach],
                (((1,), (1,)), ((), ())),
                preferred_element_type=F32,
            )
            sol[s, i // 2, :, (i % 2) * step : (i % 2 + 1) * step] = block
            for k in range(step // BLK):
                sx3[s, i * (step // BLK) + k] = block[:, k * BLK : (k + 1) * BLK]

        load_t[s].wait()

        def update(h):
            return jnp.concatenate(
                [
                    product(lambda i: sx3[s, i], lambda k: tile_pat[s, 0, h, b, k], tiles.at[s, h, b])
                    for b in range(NBR)
                ],
                axis=1,
            )

        def carried():
            if s > 0:
                arrived(cmsg.at[s - 1], c_sem.at[s - 1])
                v = cmsg[s - 1].astype(F32)
                return jnp.concatenate([v[:m], v[m:]], axis=1)
            for dl in range(1, L):
                i = leaf_at(dl)
                arrived(part1.at[i], part1_sem.at[i])
            total = part1[0].astype(F32)
            for i in range(1, L):
                total = total + part1[i].astype(F32)
            return jnp.concatenate([total[:m], total[m:]], axis=1)

        if s < S - 1:
            if s == 0:
                arrived(rhsn, rhs_sem.at[R])
            first = rhsn[s] - (update(0) + carried())
            xsend[s] = pack(first).astype(BF16)
            for dr in range(R):
                send(xsend.at[s], xmsg.at[s, r], x_sem.at[s, r], (nxt, row_at(dr), l))
            csend[s] = pack(update(1)).astype(BF16)
            send(csend.at[s], cmsg.at[s], c_sem.at[s], (nxt, r, l))
        mine[s] = pack(sol[s, r]).astype(BF16)
        load(mine.at[s], solved_all.at[s, g])
        for d in range(1, G):
            send(mine.at[s], solved_all.at[s, g], sol_sem.at[s, g], (c, r, mate(d)))
        if s == S - 1:
            for h in range(2):
                fin[h] = pack(update(h) + carried() if h == 0 else update(h)).astype(BF16)
                for d in range(G):
                    send(fin.at[h], fin_all.at[h, g], fin_sem.at[h, g], (nxt, r, mate(d)))

    for s in range(S):
        for d in range(1, G):
            j = lax.rem(g + d, G)
            arrived(solved_all.at[s, j], sol_sem.at[s, j])
    for h in range(2):
        for j in range(G):
            arrived(fin_all.at[h, j], fin_sem.at[h, j])
    for copy in loads[-S:]:
        copy.wait()
    for copy in started:
        copy.wait_send()


def unpack_kernel(m, solved_all, fin_all, solved_out, outgoing):
    half = solved_all.shape[3]
    for i in range(solved_all.shape[0]):
        for j in range(solved_all.shape[1]):
            value = solved_all[i, j].astype(F32)
            solved_out[i, 0, j * m : (j + 1) * m, :half] = value[:m]
            solved_out[i, 0, j * m : (j + 1) * m, half:] = value[m:]
    for i in range(fin_all.shape[0]):
        for j in range(fin_all.shape[1]):
            value = fin_all[i, j].astype(F32)
            outgoing[0, i, j * m : (j + 1) * m, :half] = value[:m]
            outgoing[0, i, j * m : (j + 1) * m, half:] = value[m:]


def per_device(axes, rhs_top, diag_inv, tile_vals, tile_pattern, sub_vals, sub_pattern, sub_solved):
    C, R, L = axes
    S, _, NRHS, W = rhs_top.shape
    NBR, NB, BLK = tile_vals.shape[3:6]
    PW = diag_inv.shape[3]
    SW = sub_solved.shape[3]
    G = max(1, min(L, NRHS // 8))
    m = NRHS // G
    sizes = (C, R, L, G, S, NRHS, W, BLK, NBR, NB)
    hbm = pl.BlockSpec(memory_space=pltpu.HBM)
    out = pl.BlockSpec(memory_space=pltpu.HBM)
    smem = pl.BlockSpec(memory_space=pltpu.SMEM)
    dma = pltpu.SemaphoreType.DMA
    n_sends = (
        2 * (R - 1) + 1 + (L * R - 1) + (L - 1) + (S - 1) * (R - 1) + (S - 1) * (R + 1) + S * (G - 1) + 2 * G
    )
    solved_all, fin_all = pl.pallas_call(
        functools.partial(kernel, sizes),
        out_shape=(
            jax.ShapeDtypeStruct((S, G, 2 * m, W // 2), BF16),
            jax.ShapeDtypeStruct((2, G, 2 * m, W // 2), BF16),
        ),
        in_specs=[hbm, hbm, hbm, smem, hbm, smem, hbm],
        out_specs=(out, out),
        scratch_shapes=[
            pltpu.VMEM(sub_vals.shape[2:], BF16),
            pltpu.VMEM((NRHS, SW), BF16),
            pltpu.VMEM((SW // BLK, NRHS, BLK), BF16),
            pltpu.VMEM((S,) + tile_vals.shape[2:], BF16),
            pltpu.VMEM((S, R, W, PW), BF16),
            pltpu.VMEM((R, m, W), F32),
            pltpu.VMEM((S - 1, m, W), F32),
            pltpu.VMEM((2, G, 2 * m, W // 2), BF16),
            pltpu.VMEM((L, R, 2 * m, W // 2), BF16),
            pltpu.VMEM((L, 2 * m, W // 2), BF16),
            pltpu.VMEM((S - 1, R, 2 * m, W // 2), BF16),
            pltpu.VMEM((S - 1, 2 * m, W // 2), BF16),
            pltpu.VMEM((S - 1, 2 * m, W // 2), BF16),
            pltpu.VMEM((S - 1, 2 * m, W // 2), BF16),
            pltpu.VMEM((S, PW // BLK, m, BLK), F32),
            pltpu.VMEM((S, R, m, W), F32),
            pltpu.VMEM((2, 2 * m, W // 2), BF16),
            pltpu.VMEM((S, 2 * m, W // 2), BF16),
            dma((3 + 3 * S,)),
            dma((n_sends,)),
            dma((L, R)),
            dma((L,)),
            dma((S, R)),
            dma((R + 1,)),
            dma((S - 1, R)),
            dma((S - 1,)),
            dma((S, G)),
            dma((2, G)),
        ],
        compiler_params=pltpu.CompilerParams(
            collective_id=0, has_side_effects=True, vmem_limit_bytes=56 * 1024 * 1024
        ),
    )(rhs_top, diag_inv, tile_vals, tile_pattern, sub_vals, sub_pattern, sub_solved)
    return pl.pallas_call(
        functools.partial(unpack_kernel, m),
        out_shape=(
            jax.ShapeDtypeStruct((S, 1, NRHS, W), F32),
            jax.ShapeDtypeStruct((1, 2, NRHS, W), F32),
        ),
        in_specs=[pl.BlockSpec(memory_space=pltpu.VMEM)] * 2,
        out_specs=(pl.BlockSpec(memory_space=pltpu.VMEM),) * 2,
    )(solved_all, fin_all)


def solution(mesh):
    placed = (
        P(None, "col", None, "row"),
        P(None, "col", "row", None),
        P(None, "col", None, "row", None, None, None),
        P(None, "col", None, "row", None),
        P("col", "leaf", None, "row", None, None, None),
        P("col", "leaf", None, "row", None),
        P("col", "leaf", None, None),
    )
    axes = tuple(mesh.shape[name] for name in ("col", "row", "leaf"))
    return jax.shard_map(
        functools.partial(per_device, axes),
        mesh=mesh,
        in_specs=placed,
        out_specs=(P(None, "col", None, "row"), P("col", None, None, "row")),
        check_vma=False,
    )
```

```python
import functools

import jax
import jax.numpy as jnp
from jax import lax
from jax.experimental import pallas as pl
from jax.experimental.pallas import tpu as pltpu
from jax.sharding import PartitionSpec as P

MESH = pl.DeviceIdType.MESH
F32 = jnp.float32
BF16 = jnp.bfloat16


def pack(x):
    half = x.shape[1] // 2
    return jnp.concatenate([x[:, :half], x[:, half:]], axis=0)


def kernel(
    sizes,
    rhs_hbm,
    diag_hbm,
    tile_hbm,
    tile_pat,
    sub_hbm,
    sub_pat,
    subx_hbm,
    solved_all,
    fin_all,
    subv,
    subx,
    subx3,
    tiles,
    diag,
    rhs0,
    rhsn,
    part_send,
    part0,
    part1,
    xmsg,
    xsend,
    cmsg,
    csend,
    sx3,
    sol,
    fin,
    mine,
    load_sem,
    send_sem,
    part0_sem,
    part1_sem,
    diag_sem,
    rhs_sem,
    x_sem,
    c_sem,
    sol_sem,
    fin_sem,
):
    C, R, L, G, S, NRHS, W, BLK, NBR, NB = sizes
    m = NRHS // G
    c, r, l = lax.axis_index("col"), lax.axis_index("row"), lax.axis_index("leaf")
    g = lax.rem(l, G)
    base = l - g
    nxt, prv = lax.rem(c + 1, C), lax.rem(c + C - 1, C)
    rows = pl.ds(pl.multiple_of(g * m, m), m)
    started = []

    def leaf_at(d):
        return lax.rem(l + d, L)

    def row_at(d):
        return lax.rem(r + d, R)

    def mate(d):
        return base + lax.rem(g + d, G)

    loads = []

    def load(src, dst):
        copy = pltpu.make_async_copy(src, dst, load_sem.at[len(loads)])
        copy.start()
        loads.append(copy)
        return copy

    def send(src, dst, sem, target):
        copy = pltpu.make_async_remote_copy(
            src_ref=src,
            dst_ref=dst,
            send_sem=send_sem.at[len(started)],
            recv_sem=sem,
            device_id=target,
            device_id_type=MESH,
        )
        copy.start()
        started.append(copy)

    def arrived(dst, sem):
        pltpu.make_async_remote_copy(
            src_ref=dst,
            dst_ref=dst,
            send_sem=send_sem.at[0],
            recv_sem=sem,
            device_id=(c, r, l),
            device_id_type=MESH,
        ).wait_recv()

    barrier = pltpu.get_barrier_semaphore()
    peers = []
    for dl in range(L):
        for dr in range(R):
            if dl or dr:
                peers.append((c, row_at(dr), leaf_at(dl)))
    for other in (nxt, prv):
        for dr in range(R):
            peers.append((other, row_at(dr), l))
    for peer in peers:
        pl.semaphore_signal(barrier, inc=1, device_id=peer, device_id_type=MESH)

    load_x = load(subx_hbm.at[0, 0], subx)
    load_v = load(sub_hbm.at[0, 0], subv)
    load_r = load(rhs_hbm.at[0, 0, rows], rhs0.at[r])
    load_d, load_t = [], []
    for s in range(S):
        load_d.append(load(diag_hbm.at[s, 0], diag.at[s, r]))
        load_t.append(load(tile_hbm.at[s, 0], tiles.at[s]))

    def product(lookup, pat, vals):
        lhs = jnp.concatenate([lookup(pat(k)) for k in range(NB)], axis=1)
        return jnp.dot(lhs.astype(BF16), vals[...].reshape(NB * BLK, BLK), preferred_element_type=F32)

    load_x.wait()
    for k in range(subx3.shape[0]):
        subx3[k] = subx[:, k * BLK : (k + 1) * BLK]
    load_v.wait()
    for h in range(2):
        part = jnp.concatenate(
            [
                product(lambda i: subx3[i], lambda k: sub_pat[0, 0, h, b, k], subv.at[h, b])
                for b in range(NBR)
            ],
            axis=1,
        )
        for j in range(G):
            part_send[h, j] = pack(part[j * m : (j + 1) * m]).astype(BF16)
    part0[l, r] = part_send[0, g]
    part1[l] = part_send[1, g]

    pl.semaphore_wait(barrier, len(peers))

    for dr in range(1, R):
        send(rhs_hbm.at[0, 0, rows], rhs0.at[r], rhs_sem.at[r], (c, row_at(dr), l))
    for dl in range(L):
        for dr in range(R):
            if dl or dr:
                there = leaf_at(dl)
                send(
                    part_send.at[0, lax.rem(there, G)],
                    part0.at[l, r],
                    part0_sem.at[l, r],
                    (c, row_at(dr), there),
                )
    for dr in range(1, R):
        send(diag_hbm.at[0, 0], diag.at[0, r], diag_sem.at[0, r], (c, row_at(dr), l))
    for dl in range(1, L):
        there = leaf_at(dl)
        send(part_send.at[1, lax.rem(there, G)], part1.at[l], part1_sem.at[l], (c, r, there))
    send(rhs_hbm.at[pl.ds(1, S - 1), 0, rows], rhsn, rhs_sem.at[R], (prv, r, l))
    for s in range(1, S):
        for dr in range(1, R):
            send(diag_hbm.at[s, 0], diag.at[s, r], diag_sem.at[s, r], (c, row_at(dr), l))

    load_r.wait()
    for dr in range(1, R):
        there = row_at(dr)
        arrived(rhs0.at[there], rhs_sem.at[there])
    for dl in range(L):
        for dr in range(R):
            if dl or dr:
                i, j = leaf_at(dl), row_at(dr)
                arrived(part0.at[i, j], part0_sem.at[i, j])
    pieces = []
    for j in range(R):
        total = part0[0, j].astype(F32)
        for i in range(1, L):
            total = total + part0[i, j].astype(F32)
        value = pack(rhs0[j]) - total
        pieces += [value[:m], value[m:]]

    for s in range(S):
        if s > 0:
            pieces = []
            for j in range(R):
                arrived(xmsg.at[s - 1, j], x_sem.at[s - 1, j])
                value = xmsg[s - 1, j].astype(F32)
                pieces += [value[:m], value[m:]]
        x = jnp.concatenate(pieces, axis=1).astype(BF16)
        load_d[s].wait()
        for dr in range(1, R):
            there = row_at(dr)
            arrived(diag.at[s, there], diag_sem.at[s, there])
        step = W // 2
        for i in range(2 * R):
            reach = (i + 1) * step
            block = lax.dot_general(
                x[:, :reach],
                diag[s, i // 2, (i % 2) * step : (i % 2 + 1) * step, :reach],
                (((1,), (1,)), ((), ())),
                preferred_element_type=F32,
            )
            sol[s, i // 2, :, (i % 2) * step : (i % 2 + 1) * step] = block
            for k in range(step // BLK):
                sx3[s, i * (step // BLK) + k] = block[:, k * BLK : (k + 1) * BLK]

        load_t[s].wait()

        def update(h):
            return jnp.concatenate(
                [
                    product(lambda i: sx3[s, i], lambda k: tile_pat[s, 0, h, b, k], tiles.at[s, h, b])
                    for b in range(NBR)
                ],
                axis=1,
            )

        def carried():
            if s > 0:
                arrived(cmsg.at[s - 1], c_sem.at[s - 1])
                v = cmsg[s - 1].astype(F32)
                return jnp.concatenate([v[:m], v[m:]], axis=1)
            for dl in range(1, L):
                i = leaf_at(dl)
                arrived(part1.at[i], part1_sem.at[i])
            total = part1[0].astype(F32)
            for i in range(1, L):
                total = total + part1[i].astype(F32)
            return jnp.concatenate([total[:m], total[m:]], axis=1)

        if s < S - 1:
            if s == 0:
                arrived(rhsn, rhs_sem.at[R])
            first = rhsn[s] - (update(0) + carried())
            xsend[s] = pack(first).astype(BF16)
            for dr in range(R):
                send(xsend.at[s], xmsg.at[s, r], x_sem.at[s, r], (nxt, row_at(dr), l))
            csend[s] = pack(update(1)).astype(BF16)
            send(csend.at[s], cmsg.at[s], c_sem.at[s], (nxt, r, l))
        mine[s] = pack(sol[s, r]).astype(BF16)
        load(mine.at[s], solved_all.at[s, g])
        for d in range(1, G):
            send(mine.at[s], solved_all.at[s, g], sol_sem.at[s, g], (c, r, mate(d)))
        if s == S - 1:
            for h in range(2):
                fin[h] = pack(update(h) + carried() if h == 0 else update(h)).astype(BF16)
                for d in range(G):
                    send(fin.at[h], fin_all.at[h, g], fin_sem.at[h, g], (nxt, r, mate(d)))

    for s in range(S):
        for d in range(1, G):
            j = lax.rem(g + d, G)
            arrived(solved_all.at[s, j], sol_sem.at[s, j])
    for h in range(2):
        for j in range(G):
            arrived(fin_all.at[h, j], fin_sem.at[h, j])
    for copy in loads[-S:]:
        copy.wait()
    for copy in started:
        copy.wait_send()


def unpack_kernel(m, solved_all, fin_all, solved_out, outgoing, packed, packed_fin, plain, plain_fin, sem):
    half = solved_all.shape[3]
    S, G = solved_all.shape[:2]
    fetch = [
        pltpu.make_async_copy(fin_all, packed_fin, sem.at[0]),
        pltpu.make_async_copy(solved_all, packed, sem.at[1]),
    ]
    for copy in fetch:
        copy.start()
    out = []

    def write(src, i, dst_vmem, dst):
        for j in range(G):
            value = src[i, j].astype(F32)
            dst_vmem[i, j * m : (j + 1) * m, :half] = value[:m]
            dst_vmem[i, j * m : (j + 1) * m, half:] = value[m:]
        copy = pltpu.make_async_copy(dst_vmem.at[i], dst, sem.at[2 + len(out)])
        copy.start()
        out.append(copy)

    fetch[0].wait()
    for i in range(fin_all.shape[0]):
        write(packed_fin, i, plain_fin, outgoing.at[0, i])
    fetch[1].wait()
    for i in range(S):
        write(packed, i, plain, solved_out.at[i, 0])
    for copy in out:
        copy.wait()


def per_device(axes, rhs_top, diag_inv, tile_vals, tile_pattern, sub_vals, sub_pattern, sub_solved):
    C, R, L = axes
    S, _, NRHS, W = rhs_top.shape
    NBR, NB, BLK = tile_vals.shape[3:6]
    PW = diag_inv.shape[3]
    SW = sub_solved.shape[3]
    G = max(1, min(L, NRHS // 8))
    m = NRHS // G
    sizes = (C, R, L, G, S, NRHS, W, BLK, NBR, NB)
    hbm = pl.BlockSpec(memory_space=pltpu.HBM)
    out = pl.BlockSpec(memory_space=pltpu.HBM)
    smem = pl.BlockSpec(memory_space=pltpu.SMEM)
    dma = pltpu.SemaphoreType.DMA
    n_sends = (
        2 * (R - 1) + 1 + (L * R - 1) + (L - 1) + (S - 1) * (R - 1) + (S - 1) * (R + 1) + S * (G - 1) + 2 * G
    )
    solved_all, fin_all = pl.pallas_call(
        functools.partial(kernel, sizes),
        out_shape=(
            jax.ShapeDtypeStruct((S, G, 2 * m, W // 2), BF16),
            jax.ShapeDtypeStruct((2, G, 2 * m, W // 2), BF16),
        ),
        in_specs=[hbm, hbm, hbm, smem, hbm, smem, hbm],
        out_specs=(out, out),
        scratch_shapes=[
            pltpu.VMEM(sub_vals.shape[2:], BF16),
            pltpu.VMEM((NRHS, SW), BF16),
            pltpu.VMEM((SW // BLK, NRHS, BLK), BF16),
            pltpu.VMEM((S,) + tile_vals.shape[2:], BF16),
            pltpu.VMEM((S, R, W, PW), BF16),
            pltpu.VMEM((R, m, W), F32),
            pltpu.VMEM((S - 1, m, W), F32),
            pltpu.VMEM((2, G, 2 * m, W // 2), BF16),
            pltpu.VMEM((L, R, 2 * m, W // 2), BF16),
            pltpu.VMEM((L, 2 * m, W // 2), BF16),
            pltpu.VMEM((S - 1, R, 2 * m, W // 2), BF16),
            pltpu.VMEM((S - 1, 2 * m, W // 2), BF16),
            pltpu.VMEM((S - 1, 2 * m, W // 2), BF16),
            pltpu.VMEM((S - 1, 2 * m, W // 2), BF16),
            pltpu.VMEM((S, PW // BLK, m, BLK), F32),
            pltpu.VMEM((S, R, m, W), F32),
            pltpu.VMEM((2, 2 * m, W // 2), BF16),
            pltpu.VMEM((S, 2 * m, W // 2), BF16),
            dma((3 + 3 * S,)),
            dma((n_sends,)),
            dma((L, R)),
            dma((L,)),
            dma((S, R)),
            dma((R + 1,)),
            dma((S - 1, R)),
            dma((S - 1,)),
            dma((S, G)),
            dma((2, G)),
        ],
        compiler_params=pltpu.CompilerParams(
            collective_id=0, has_side_effects=True, vmem_limit_bytes=56 * 1024 * 1024
        ),
    )(rhs_top, diag_inv, tile_vals, tile_pattern, sub_vals, sub_pattern, sub_solved)
    return pl.pallas_call(
        functools.partial(unpack_kernel, m),
        out_shape=(
            jax.ShapeDtypeStruct((S, 1, NRHS, W), F32),
            jax.ShapeDtypeStruct((1, 2, NRHS, W), F32),
        ),
        in_specs=[hbm] * 2,
        out_specs=(hbm,) * 2,
        scratch_shapes=[
            pltpu.VMEM(solved_all.shape, BF16),
            pltpu.VMEM(fin_all.shape, BF16),
            pltpu.VMEM((S, NRHS, W), F32),
            pltpu.VMEM((2, NRHS, W), F32),
            dma((S + 4,)),
        ],
    )(solved_all, fin_all)


def solution(mesh):
    placed = (
        P(None, "col", None, "row"),
        P(None, "col", "row", None),
        P(None, "col", None, "row", None, None, None),
        P(None, "col", None, "row", None),
        P("col", "leaf", None, "row", None, None, None),
        P("col", "leaf", None, "row", None),
        P("col", "leaf", None, None),
    )
    axes = tuple(mesh.shape[name] for name in ("col", "row", "leaf"))
    return jax.shard_map(
        functools.partial(per_device, axes),
        mesh=mesh,
        in_specs=placed,
        out_specs=(P(None, "col", None, "row"), P("col", None, None, "row")),
        check_vma=False,
    )
```
